32 devices in a mesh: dom: 4 (over x, core), band: 8 (over z, y).
Axes of the slice: x: 2, y: 2, z: 4, core: 2. Of those that a mesh axis runs over, the one named last changes fastest.
Arguments:
- orbitals: bfloat16 [1024, 4, 2, 16, 128], P('band', 'dom'), may hold values from -6 to 6
- potential: float32 [4, 2, 16, 128], P('dom'), may hold values from -1 to 1
- ritz: bfloat16 [1024, 1024], P(None, 'band'), may hold values from -0.1875 to 0.1875
Outputs:
- rotated: float32 [1024, 4, 2, 16, 128], P('band', 'dom')
The draws below stay inside these ranges and needn't reach their ends.
All inputs are finite; a program needn't handle non-finite values.
Results may differ from the reference program's by a relative error of at most 0.0029.
Values may be sent and summed in bfloat16 or wider, within the bound.
A program may use at most 64 MiB of HBM per device.

```python
import math
import jax
import jax.numpy as jnp
from jax import lax

NB = 1024
CX = 2
CY = 16
NZ = 128
DEG = 4
N_DOM = 4


def level_of(rng, shape, shards, least, top_value):
    def one(position, blocks):
        steps = jax.random.uniform(jax.random.fold_in(jax.random.fold_in(rng, 6), position), (blocks,), jnp.float32, least / len(shards), top_value / len(shards))
        return jnp.repeat(jnp.exp(steps), shape[position] // blocks).reshape((-1,) + (1,) * (len(shape) - position - 1))

    factor_of = one(*shards[0])
    for cut in shards[1:]:
        factor_of = factor_of * one(*cut)
    return factor_of


def normal_values(stream_key, shape, deviation, bound, pieces=(), kind=jnp.bfloat16):
    drawn = deviation * jax.random.normal(stream_key, shape, jnp.float32)
    if pieces:
        drawn = drawn * level_of(stream_key, shape, pieces, -0.22, 0.18)
    return jnp.clip(drawn, -bound, bound).astype(kind)


def setup_inputs(seed: int = 0) -> dict:
    splits = jax.random.split(jax.random.key(seed), 4)
    orbitals = normal_values(splits[0], (NB, N_DOM, CX, CY, NZ), 1.0, 6.0, ((0, 8), (1, 4)))
    potential = jnp.clip(jax.random.uniform(splits[1], (N_DOM, CX, CY, NZ), jnp.float32, -1.0, 1.0) * level_of(splits[1], (N_DOM, CX, CY, NZ), ((0, 4),), -0.4, 0.0), -1.0, 1.0)
    ritz = normal_values(splits[2], (NB, NB), NB ** -0.5, 0.1875, ((1, 8),))
    return dict(orbitals=orbitals, potential=potential, ritz=ritz)


lower_bound = -1.5
cut_off = 1.0
upper_bound = 9.5
coef_zero = -2.5
coef_one = 4.0 / 3.0
coef_two = -1.0 / 12.0

def filter_weights(degree):
    half_width = (upper_bound - cut_off) / 2.0
    centre = (upper_bound + cut_off) / 2.0
    sigma_now = half_width / (lower_bound - centre)
    first_scale = sigma_now / half_width
    inverse_gain = 2.0 / sigma_now
    weights = []
    for degree_step in range(1, degree):
        sigma_next = 1.0 / (inverse_gain - sigma_now)
        weights.append((2.0 * sigma_next / half_width, sigma_now * sigma_next))
        sigma_now = sigma_next
    return (centre, first_scale, weights)

def second_along(grid, axis):
    near_sum = jnp.roll(grid, 1, axis) + jnp.roll(grid, -1, axis)
    far_sum = jnp.roll(grid, 2, axis) + jnp.roll(grid, -2, axis)
    return coef_one * near_sum + coef_two * far_sum

def hamiltonian(grid, grid_pot):
    second = 3.0 * coef_zero * grid + second_along(grid, 1) + second_along(grid, 2) + second_along(grid, 3)
    return -0.5 * second + grid_pot * grid

def reference(orbitals, potential, ritz):
    grid_side = math.isqrt(N_DOM)
    block_size = math.gcd(NB, 64)
    centre, first_scale, weights = filter_weights(DEG)
    grid_pot = potential.reshape(grid_side, grid_side, CX, CY, NZ).transpose(0, 2, 1, 3, 4)
    grid_pot = grid_pot.reshape(grid_side * CX, grid_side * CY, NZ)
    grid_orb = orbitals.reshape(NB, grid_side, grid_side, CX, CY, NZ).transpose(0, 1, 3, 2, 4, 5)
    grid_orb = grid_orb.reshape(NB // block_size, block_size, grid_side * CX, grid_side * CY, NZ)

    def filter_block(start_block):
        previous = start_block.astype(jnp.float32)
        current = (hamiltonian(previous, grid_pot) - centre * previous) * first_scale
        for scale_h, scale_x in weights:
            following = (hamiltonian(current, grid_pot) - centre * current) * scale_h - scale_x * previous
            previous, current = (current, following)
        return current.astype(jnp.bfloat16)
    filtered = lax.map(filter_block, grid_orb)
    rotated = jnp.dot(ritz.T, filtered.reshape(NB, -1), preferred_element_type=jnp.float32)
    rotated = rotated.reshape(NB, grid_side, CX, grid_side, CY, NZ).transpose(0, 1, 3, 2, 4, 5)
    return rotated.reshape(NB, N_DOM, CX, CY, NZ)
```

```python
import functools
import math

import jax
import jax.numpy as jnp
from jax import lax
from jax.experimental import pallas as pl
from jax.experimental.pallas import tpu as pltpu
from jax.sharding import PartitionSpec as P

DEG = 4

lower_bound = -1.5
cut_off = 1.0
upper_bound = 9.5
coef_zero = -2.5
coef_one = 4.0 / 3.0
coef_two = -1.0 / 12.0


def filter_weights(degree):
    half_width = (upper_bound - cut_off) / 2.0
    centre = (upper_bound + cut_off) / 2.0
    sigma_now = half_width / (lower_bound - centre)
    first_scale = sigma_now / half_width
    inverse_gain = 2.0 / sigma_now
    weights = []
    for degree_step in range(1, degree):
        sigma_next = 1.0 / (inverse_gain - sigma_now)
        weights.append((2.0 * sigma_next / half_width, sigma_now * sigma_next))
        sigma_now = sigma_next
    return (centre, first_scale, weights)


def filter_kernel(side, cells_x, cells_y, in_ref, pot_ref, out_ref, even, odd):
    count_x, count_y = even.shape[0], even.shape[1]
    centre, first_scale, weights = filter_weights(DEG)
    diagonal = -0.5 * 3.0 * coef_zero - centre

    def block_of(x, y):
        dom = (x // cells_x) * side + y // cells_y
        row = (x % cells_x) * cells_y + y % cells_y
        return dom, row

    def load(y, x):
        dom, row = block_of(x, y)
        even[x, y] = in_ref[dom, row].astype(jnp.float32)

    for x in range(count_x):
        lax.fori_loop(0, count_y, lambda y, c, x=x: (load(y, x), c)[1], 0, unroll=4)

    def step(source, target, scale_h, scale_x, last):
        def row_step(y, x):
            at = lambda dx, dy: source[(x + dx) % count_x, lax.rem(y + dy + count_y, count_y)]
            here = source[x, y]
            near = (
                at(1, 0)
                + at(-1, 0)
                + (at(0, 1) + at(0, -1))
                + (pltpu.roll(here, 1, 1) + pltpu.roll(here, 127, 1))
            )
            far = (
                at(2, 0)
                + at(-2, 0)
                + (at(0, 2) + at(0, -2))
                + (pltpu.roll(here, 2, 1) + pltpu.roll(here, 126, 1))
            )
            dom, row = block_of(x, y)
            pot = pot_ref[dom, pl.ds(row, 1), :] + diagonal
            value = (pot * scale_h) * here + (
                (-0.5 * coef_one * scale_h) * near + (-0.5 * coef_two * scale_h) * far
            )
            if scale_x is not None:
                value = value - scale_x * target[x, y]
            if last:
                out_ref[dom, row] = value.astype(out_ref.dtype)
            else:
                target[x, y] = value

        for x in range(count_x):
            lax.fori_loop(0, count_y, lambda y, c, x=x: (row_step(y, x), c)[1], 0, unroll=4)

    step(even, odd, first_scale, None, False)
    source, target = odd, even
    for index, (scale_h, scale_x) in enumerate(weights):
        step(source, target, scale_h, scale_x, index == len(weights) - 1)
        source, target = target, source


def filter_bands(blocks, potential, side, cells_x, cells_y):
    doms, rows, bands, lanes = blocks.shape
    return pl.pallas_call(
        functools.partial(filter_kernel, side, cells_x, cells_y),
        out_shape=jax.ShapeDtypeStruct(blocks.shape, jnp.bfloat16),
        in_specs=[pl.BlockSpec(memory_space=pltpu.VMEM)] * 2,
        out_specs=pl.BlockSpec(memory_space=pltpu.VMEM),
        scratch_shapes=[
            pltpu.VMEM((side * cells_x, side * cells_y, bands, lanes), jnp.float32),
            pltpu.VMEM((side * cells_x, side * cells_y, bands, lanes), jnp.float32),
        ],
        compiler_params=pltpu.CompilerParams(vmem_limit_bytes=40 * 2**20),
        name="chebyshev",
    )(blocks, potential)


def on_device(orbitals, potential, ritz):
    doms = lax.axis_size("dom")
    groups = lax.axis_size("band")
    side = math.isqrt(doms)
    bands, _, cells_x, cells_y, lanes = orbitals.shape
    rows = cells_x * cells_y
    share = bands // doms
    full_ritz = lax.all_gather(ritz, "band", axis=1, tiled=True)
    full_pot = lax.all_gather(potential.reshape(1, rows, lanes), "dom", axis=0, tiled=True)
    panel = orbitals.reshape(bands, rows, lanes).transpose(1, 0, 2)
    panel = panel.reshape(rows, doms, share, lanes).transpose(1, 0, 2, 3)
    whole = lax.all_to_all(panel, "dom", split_axis=0, concat_axis=0, tiled=True)
    filtered = filter_bands(whole, full_pot, side, cells_x, cells_y)
    part = rows // groups
    pieces = filtered.reshape(doms, groups, part, share, lanes).transpose(1, 0, 2, 3, 4)
    pieces = pieces.reshape(groups * doms, part, share, lanes)
    block = lax.all_to_all(pieces, ("band", "dom"), split_axis=0, concat_axis=0, tiled=True)
    block = block.transpose(0, 2, 1, 3).reshape(groups * bands, part * lanes)
    mixed = lax.dot_general(
        full_ritz, block, (((0,), (0,)), ((), ())), preferred_element_type=jnp.float32
    )
    mixed = mixed.astype(jnp.bfloat16).reshape(groups, bands, part, lanes)
    returned = lax.all_to_all(mixed, "band", split_axis=0, concat_axis=0, tiled=True)
    rotated = returned.transpose(1, 0, 2, 3).reshape(bands, rows, lanes)
    return rotated.astype(jnp.float32).reshape(orbitals.shape)


def solution(mesh):
    in_specs = (P("band", "dom", None, None, None), P("dom", None, None, None), P(None, "band"))
    out_specs = P("band", "dom", None, None, None)
    return jax.shard_map(
        on_device, mesh=mesh, in_specs=in_specs, out_specs=out_specs, check_vma=False
    )
```

```python
import functools
import math

import jax
import jax.numpy as jnp
from jax import lax
from jax.experimental import pallas as pl
from jax.experimental.pallas import tpu as pltpu
from jax.sharding import PartitionSpec as P

DEG = 4

lower_bound = -1.5
cut_off = 1.0
upper_bound = 9.5
coef_zero = -2.5
coef_one = 4.0 / 3.0
coef_two = -1.0 / 12.0


def filter_weights(degree):
    half_width = (upper_bound - cut_off) / 2.0
    centre = (upper_bound + cut_off) / 2.0
    sigma_now = half_width / (lower_bound - centre)
    first_scale = sigma_now / half_width
    inverse_gain = 2.0 / sigma_now
    weights = []
    for degree_step in range(1, degree):
        sigma_next = 1.0 / (inverse_gain - sigma_now)
        weights.append((2.0 * sigma_next / half_width, sigma_now * sigma_next))
        sigma_now = sigma_next
    return (centre, first_scale, weights)


def peer_of(index, doms):
    return {"band": lax.div(index, doms), "dom": lax.rem(index, doms)}


def loop(low, high, body, unroll=None):
    lax.fori_loop(low, high, lambda i, c: (body(i), c)[1], 0, unroll=unroll)


def filter_kernel(
    side, cells_x, cells_y, doms, groups,
    panel, pot_in, out_ref,
    pot_ref, got, done, even, odd,
    send_p, recv_p, here_p, send_a, recv_a, here_a, send_b, recv_b, here_b,
):
    chunks = panel.shape[0]
    count_x, count_y = even.shape[0], even.shape[1]
    part = out_ref.shape[2]
    total = doms * groups
    my_dom, my_group = lax.axis_index("dom"), lax.axis_index("band")
    me = my_group * doms + my_dom
    centre, first_scale, weights = filter_weights(DEG)
    diagonal = -0.5 * 3.0 * coef_zero - centre

    barrier = pltpu.get_barrier_semaphore()

    def greet(offset):
        pl.semaphore_signal(
            barrier, inc=1, device_id=peer_of(lax.rem(me + offset, total), doms),
            device_id_type=pl.DeviceIdType.MESH,
        )

    loop(1, total, greet)
    pl.semaphore_wait(barrier, total - 1)

    def copy_p(target, source):
        return pltpu.make_async_remote_copy(
            src_ref=pot_in,
            dst_ref=pot_ref.at[source],
            send_sem=send_p.at[target],
            recv_sem=recv_p.at[source],
            device_id={"dom": target},
            device_id_type=pl.DeviceIdType.MESH,
        )

    def copy_a(chunk, target, source):
        return pltpu.make_async_remote_copy(
            src_ref=panel.at[chunk, target],
            dst_ref=got.at[chunk, source],
            send_sem=send_a.at[chunk, target],
            recv_sem=recv_a.at[chunk, source],
            device_id={"dom": target},
            device_id_type=pl.DeviceIdType.MESH,
        )

    def copy_b(chunk, target, source):
        group, dom = lax.div(target, doms), lax.rem(target, doms)
        return pltpu.make_async_remote_copy(
            src_ref=done.at[chunk, dom, pl.ds(group * part, part)],
            dst_ref=out_ref.at[chunk, source],
            send_sem=send_b.at[chunk, target],
            recv_sem=recv_b.at[chunk, source],
            device_id=peer_of(target, doms),
            device_id_type=pl.DeviceIdType.MESH,
        )

    def local_a(chunk):
        return pltpu.make_async_copy(
            panel.at[chunk, my_dom], got.at[chunk, my_dom], here_a.at[chunk]
        )

    def local_b(chunk):
        return pltpu.make_async_copy(
            done.at[chunk, my_dom, pl.ds(my_group * part, part)],
            out_ref.at[chunk, me], here_b.at[chunk],
        )

    def other_dom(offset):
        return lax.rem(my_dom + offset, doms)

    def other(offset):
        return lax.rem(me + offset, total)

    def start_a(chunk):
        local_a(chunk).start()
        loop(1, doms, lambda o: copy_a(chunk, other_dom(o), my_dom).start())

    local_p = pltpu.make_async_copy(pot_in, pot_ref.at[my_dom], here_p)
    local_p.start()
    loop(1, doms, lambda o: copy_p(other_dom(o), my_dom).start())
    loop(0, chunks, start_a)
    local_p.wait()
    loop(1, doms, lambda o: copy_p(my_dom, other_dom(o)).wait_recv())

    def block_of(x, y):
        dom = (x // cells_x) * side + lax.div(y, cells_y)
        row = (x % cells_x) * cells_y + lax.rem(y, cells_y)
        return dom, row

    def load(chunk, y):
        for x in range(count_x):
            dom, row = block_of(x, y)
            even[x, y] = got[chunk, dom, row].astype(jnp.float32)

    def step(chunk, source, target, scale_h, scale_x, last):
        def row_step(y):
            at = lambda dy: lax.rem(y + dy + count_y, count_y)
            low, lower, high, higher = at(-1), at(-2), at(1), at(2)
            rows = [source[x, y] for x in range(count_x)]
            for x in range(count_x):
                here = rows[x]
                near = (
                    (rows[(x + 1) % count_x] + rows[(x - 1) % count_x])
                    + (source[x, low] + source[x, high])
                    + (pltpu.roll(here, 1, 1) + pltpu.roll(here, 127, 1))
                )
                far = (
                    (rows[(x + 2) % count_x] + rows[(x - 2) % count_x])
                    + (source[x, lower] + source[x, higher])
                    + (pltpu.roll(here, 2, 1) + pltpu.roll(here, 126, 1))
                )
                dom, row = block_of(x, y)
                pot = pot_ref[dom, pl.ds(row, 1), :] + diagonal
                value = (pot * scale_h) * here + (
                    (-0.5 * coef_one * scale_h) * near + (-0.5 * coef_two * scale_h) * far
                )
                if scale_x is not None:
                    value = value - scale_x * target[x, y]
                if last:
                    done[chunk, dom, row] = value.astype(done.dtype)
                else:
                    target[x, y] = value

        loop(0, count_y, row_step, unroll=2)

    def work(chunk):
        local_a(chunk).wait()
        loop(1, doms, lambda o: copy_a(chunk, my_dom, other_dom(o)).wait_recv())
        loop(0, count_y, lambda y: load(chunk, y), unroll=2)
        step(chunk, even, odd, first_scale, None, False)
        source, target = odd, even
        for index, (scale_h, scale_x) in enumerate(weights):
            step(chunk, source, target, scale_h, scale_x, index == len(weights) - 1)
            source, target = target, source
        loop(1, total, lambda o: copy_b(chunk, other(o), me).start())
        local_b(chunk).start()

    loop(0, chunks, work)

    loop(1, doms, lambda o: copy_p(other_dom(o), my_dom).wait_send())

    def finish(chunk):
        loop(1, doms, lambda o: copy_a(chunk, other_dom(o), my_dom).wait_send())
        local_b(chunk).wait()
        loop(1, total, lambda o: copy_b(chunk, other(o), me).wait_send())
        loop(1, total, lambda o: copy_b(chunk, other(o), other(o)).wait_recv())

    loop(0, chunks, finish)


def filter_bands(panel, potential, side, cells_x, cells_y, groups):
    chunks, doms, rows, bands, lanes = panel.shape
    total, part = doms * groups, rows // groups
    field = (side * cells_x, side * cells_y, bands, lanes)
    dma = pltpu.SemaphoreType.DMA
    return pl.pallas_call(
        functools.partial(filter_kernel, side, cells_x, cells_y, doms, groups),
        out_shape=jax.ShapeDtypeStruct((chunks, total, part, bands, lanes), jnp.bfloat16),
        in_specs=[pl.BlockSpec(memory_space=pltpu.VMEM)] * 2,
        out_specs=pl.BlockSpec(memory_space=pltpu.VMEM),
        scratch_shapes=[
            pltpu.VMEM((doms,) + potential.shape, jnp.float32),
            pltpu.VMEM(panel.shape, jnp.bfloat16),
            pltpu.VMEM(panel.shape, jnp.bfloat16),
            pltpu.VMEM(field, jnp.float32),
            pltpu.VMEM(field, jnp.float32),
            dma((doms,)),
            dma((doms,)),
            dma,
            dma((chunks, doms)),
            dma((chunks, doms)),
            dma((chunks,)),
            dma((chunks, total)),
            dma((chunks, total)),
            dma((chunks,)),
        ],
        compiler_params=pltpu.CompilerParams(
            vmem_limit_bytes=40 * 2**20, collective_id=0, has_side_effects=True
        ),
        name="chebyshev",
    )(panel, potential)


def on_device(orbitals, potential, ritz):
    doms = lax.axis_size("dom")
    groups = lax.axis_size("band")
    side = math.isqrt(doms)
    bands, _, cells_x, cells_y, lanes = orbitals.shape
    rows = cells_x * cells_y
    share = bands // doms
    deep = min(share, 16)
    chunks = share // deep
    part = rows // groups
    full_ritz = lax.all_gather(ritz, "band", axis=1, tiled=True)
    panel = orbitals.reshape(doms, chunks, deep, rows, lanes).transpose(1, 0, 3, 2, 4)
    block = filter_bands(panel, potential.reshape(rows, lanes), side, cells_x, cells_y, groups)
    block = block.reshape(chunks, groups * doms, part, deep, lanes).transpose(1, 0, 3, 2, 4)
    block = block.reshape(groups * bands, part * lanes)
    mixed = lax.dot_general(
        full_ritz, block, (((0,), (0,)), ((), ())), preferred_element_type=jnp.float32
    )
    mixed = mixed.astype(jnp.bfloat16).reshape(groups, bands, part, lanes)
    returned = lax.all_to_all(mixed, "band", split_axis=0, concat_axis=0, tiled=True)
    rotated = returned.transpose(1, 0, 2, 3).reshape(bands, rows, lanes)
    return rotated.astype(jnp.float32).reshape(orbitals.shape)


def solution(mesh):
    in_specs = (P("band", "dom", None, None, None), P("dom", None, None, None), P(None, "band"))
    out_specs = P("band", "dom", None, None, None)
    return jax.shard_map(
        on_device, mesh=mesh, in_specs=in_specs, out_specs=out_specs, check_vma=False
    )
```

```python
import functools
import math

import jax
import jax.numpy as jnp
from jax import lax
from jax.experimental import pallas as pl
from jax.experimental.pallas import tpu as pltpu
from jax.sharding import PartitionSpec as P

DEG = 4

lower_bound = -1.5
cut_off = 1.0
upper_bound = 9.5
coef_zero = -2.5
coef_one = 4.0 / 3.0
coef_two = -1.0 / 12.0


def filter_weights(degree):
    half_width = (upper_bound - cut_off) / 2.0
    centre = (upper_bound + cut_off) / 2.0
    sigma_now = half_width / (lower_bound - centre)
    first_scale = sigma_now / half_width
    inverse_gain = 2.0 / sigma_now
    weights = []
    for degree_step in range(1, degree):
        sigma_next = 1.0 / (inverse_gain - sigma_now)
        weights.append((2.0 * sigma_next / half_width, sigma_now * sigma_next))
        sigma_now = sigma_next
    return (centre, first_scale, weights)


def peer_of(index, doms):
    return {"band": lax.div(index, doms), "dom": lax.rem(index, doms)}


def loop(low, high, body, unroll=None):
    lax.fori_loop(low, high, lambda i, c: (body(i), c)[1], 0, unroll=unroll)


QUARTERS = 4


def filter_kernel(side, cells_x, cells_y, doms, groups, fused, *refs):
    if fused:
        panel, pot_in, ritz_in, final = refs[:4]
        out_ref, ritz_all, mixed, send_r, recv_r, here_r, send_x, recv_x, send_d, recv_d, here_d = refs[-11:]
        refs = refs[4:-11]
    else:
        panel, pot_in, out_ref = refs[:3]
        refs = refs[3:]
    pot_ref, got, done, even, odd = refs[:5]
    send_p, recv_p, here_p, send_a, recv_a, here_a, send_b, recv_b, here_b = refs[5:]
    chunks = panel.shape[0]
    count_x, count_y = even.shape[0], even.shape[1]
    part = out_ref.shape[2]
    total = doms * groups
    my_dom, my_group = lax.axis_index("dom"), lax.axis_index("band")
    me = my_group * doms + my_dom
    centre, first_scale, weights = filter_weights(DEG)
    diagonal = -0.5 * 3.0 * coef_zero - centre

    barrier = pltpu.get_barrier_semaphore()

    def greet(offset):
        pl.semaphore_signal(
            barrier, inc=1, device_id=peer_of(lax.rem(me + offset, total), doms),
            device_id_type=pl.DeviceIdType.MESH,
        )

    loop(1, total, greet)
    pl.semaphore_wait(barrier, total - 1)

    def copy_p(target, source):
        return pltpu.make_async_remote_copy(
            src_ref=pot_in,
            dst_ref=pot_ref.at[source],
            send_sem=send_p.at[target],
            recv_sem=recv_p.at[source],
            device_id={"dom": target},
            device_id_type=pl.DeviceIdType.MESH,
        )

    def copy_a(chunk, target, source):
        return pltpu.make_async_remote_copy(
            src_ref=panel.at[chunk, target],
            dst_ref=got.at[chunk, source],
            send_sem=send_a.at[chunk, target],
            recv_sem=recv_a.at[chunk, source],
            device_id={"dom": target},
            device_id_type=pl.DeviceIdType.MESH,
        )

    def copy_b(chunk, target, source):
        group, dom = lax.div(target, doms), lax.rem(target, doms)
        return pltpu.make_async_remote_copy(
            src_ref=done.at[chunk, dom, pl.ds(group * part, part)],
            dst_ref=out_ref.at[chunk, source],
            send_sem=send_b.at[chunk, target],
            recv_sem=recv_b.at[chunk, source],
            device_id=peer_of(target, doms),
            device_id_type=pl.DeviceIdType.MESH,
        )

    def local_a(chunk):
        return pltpu.make_async_copy(
            panel.at[chunk, my_dom], got.at[chunk, my_dom], here_a.at[chunk]
        )

    def local_b(chunk):
        return pltpu.make_async_copy(
            done.at[chunk, my_dom, pl.ds(my_group * part, part)],
            out_ref.at[chunk, me], here_b.at[chunk],
        )

    def other_dom(offset):
        return lax.rem(my_dom + offset, doms)

    def other(offset):
        return lax.rem(me + offset, total)

    def start_a(chunk):
        local_a(chunk).start()
        loop(1, doms, lambda o: copy_a(chunk, other_dom(o), my_dom).start())

    local_p = pltpu.make_async_copy(pot_in, pot_ref.at[my_dom], here_p)
    local_p.start()
    loop(1, doms, lambda o: copy_p(other_dom(o), my_dom).start())
    loop(0, chunks, start_a)
    if fused:
        wide = ritz_in.shape[1]
        quarter = lax.rem(my_dom, QUARTERS)
        base = my_dom - quarter
        across = lax.rem(quarter + 2, QUARTERS)
        beside = quarter + 1 - 2 * lax.rem(quarter, 2)
        opposite = lax.rem(beside + 2, QUARTERS)

        def other_group(offset):
            return lax.rem(my_group + offset, groups)

        def copy_r(target, source):
            return pltpu.make_async_remote_copy(
                src_ref=ritz_in.at[quarter],
                dst_ref=ritz_all.at[quarter, pl.ds(pl.multiple_of(source * wide, wide), wide)],
                send_sem=send_r.at[target],
                recv_sem=recv_r.at[source],
                device_id={"band": target},
                device_id_type=pl.DeviceIdType.MESH,
            )

        def copy_x(which, index, target):
            return pltpu.make_async_remote_copy(
                src_ref=ritz_all.at[index],
                dst_ref=ritz_all.at[index],
                send_sem=send_x.at[which],
                recv_sem=recv_x.at[which],
                device_id={"dom": base + target},
                device_id_type=pl.DeviceIdType.MESH,
            )

        local_r = pltpu.make_async_copy(
            ritz_in.at[quarter],
            ritz_all.at[quarter, pl.ds(pl.multiple_of(my_group * wide, wide), wide)],
            here_r,
        )
        local_r.start()
        loop(1, groups, lambda o: copy_r(other_group(o), my_group).start())
    local_p.wait()
    loop(1, doms, lambda o: copy_p(my_dom, other_dom(o)).wait_recv())

    def block_of(x, y):
        dom = (x // cells_x) * side + lax.div(y, cells_y)
        row = (x % cells_x) * cells_y + lax.rem(y, cells_y)
        return dom, row

    def load(chunk, y):
        for x in range(count_x):
            dom, row = block_of(x, y)
            even[x, y] = got[chunk, dom, row].astype(jnp.float32)

    def step(chunk, source, target, scale_h, scale_x, last):
        def row_step(y):
            at = lambda dy: lax.rem(y + dy + count_y, count_y)
            low, lower, high, higher = at(-1), at(-2), at(1), at(2)
            rows = [source[x, y] for x in range(count_x)]
            for x in range(count_x):
                here = rows[x]
                near = (
                    (rows[(x + 1) % count_x] + rows[(x - 1) % count_x])
                    + (source[x, low] + source[x, high])
                    + (pltpu.roll(here, 1, 1) + pltpu.roll(here, 127, 1))
                )
                far = (
                    (rows[(x + 2) % count_x] + rows[(x - 2) % count_x])
                    + (source[x, lower] + source[x, higher])
                    + (pltpu.roll(here, 2, 1) + pltpu.roll(here, 126, 1))
                )
                dom, row = block_of(x, y)
                pot = pot_ref[dom, pl.ds(row, 1), :] + diagonal
                value = (pot * scale_h) * here + (
                    (-0.5 * coef_one * scale_h) * near + (-0.5 * coef_two * scale_h) * far
                )
                if scale_x is not None:
                    value = value - scale_x * target[x, y]
                if last:
                    done[chunk, dom, row] = value.astype(done.dtype)
                else:
                    target[x, y] = value

        loop(0, count_y, row_step, unroll=2)

    def work(chunk):
        local_a(chunk).wait()
        loop(1, doms, lambda o: copy_a(chunk, my_dom, other_dom(o)).wait_recv())
        loop(0, count_y, lambda y: load(chunk, y), unroll=2)
        step(chunk, even, odd, first_scale, None, False)
        source, target = odd, even
        for index, (scale_h, scale_x) in enumerate(weights):
            step(chunk, source, target, scale_h, scale_x, index == len(weights) - 1)
            source, target = target, source
        loop(1, total, lambda o: copy_b(chunk, other(o), me).start())
        local_b(chunk).start()

    if fused:
        loop(0, 1, work)
        local_r.wait()
        loop(1, groups, lambda o: copy_r(my_group, other_group(o)).wait_recv())
        copy_x(0, quarter, across).start()
        copy_x(1, quarter, beside).start()
        loop(1, chunks, work)
        copy_x(0, across, across).wait_recv()
        copy_x(2, across, beside).start()
        loop(1, groups, lambda o: copy_r(other_group(o), my_group).wait_send())
        copy_x(1, beside, beside).wait_recv()
        copy_x(2, opposite, beside).wait_recv()
    else:
        loop(0, chunks, work)

    loop(1, doms, lambda o: copy_p(other_dom(o), my_dom).wait_send())

    def finish(chunk):
        loop(1, doms, lambda o: copy_a(chunk, other_dom(o), my_dom).wait_send())
        local_b(chunk).wait()
        loop(1, total, lambda o: copy_b(chunk, other(o), me).wait_send())
        loop(1, total, lambda o: copy_b(chunk, other(o), other(o)).wait_recv())

    loop(0, chunks, finish)
    if not fused:
        return
    copy_x(0, quarter, across).wait_send()
    copy_x(1, quarter, beside).wait_send()
    copy_x(2, across, beside).wait_send()

    halves, pair = mixed.shape[0], mixed.shape[1]
    deep, lanes = out_ref.shape[3], out_ref.shape[4]
    depth = ritz_all.shape[2]
    devices = depth // deep

    def copy_d(half, target, source):
        return pltpu.make_async_remote_copy(
            src_ref=mixed.at[half, :, pl.ds(pl.multiple_of(target * wide, wide), wide)],
            dst_ref=final.at[source, pl.ds(half * pair, pair)],
            send_sem=send_d.at[half, target],
            recv_sem=recv_d.at[half, source],
            device_id={"band": target},
            device_id_type=pl.DeviceIdType.MESH,
        )

    def local_d(half):
        return pltpu.make_async_copy(
            mixed.at[half, :, pl.ds(pl.multiple_of(my_group * wide, wide), wide)],
            final.at[my_group, pl.ds(half * pair, pair)], here_d.at[half],
        )

    for half in range(halves):
        columns = []
        for q in range(QUARTERS):
            chunk, first = (q * devices) // total, (q * devices) % total
            pieces = [
                out_ref[chunk, first : first + devices, half * pair + r].reshape(depth, lanes)
                for r in range(pair)
            ]
            columns.append(jnp.concatenate(pieces, axis=1))

        def rotate(g):
            rows = pl.ds(pl.multiple_of(g * 256, 256), 256)
            value = jnp.dot(ritz_all[0, rows, :], columns[0], preferred_element_type=jnp.float32)
            for q in range(1, QUARTERS):
                value = value + jnp.dot(
                    ritz_all[q, rows, :], columns[q], preferred_element_type=jnp.float32
                )
            for r in range(pair):
                mixed[half, r, rows, :] = value[:, r * lanes : (r + 1) * lanes].astype(mixed.dtype)

        for g in range(ritz_all.shape[1] // 256):
            rotate(g)
        loop(1, groups, lambda o: copy_d(half, other_group(o), my_group).start())
        local_d(half).start()

    def receive(half):
        local_d(half).wait()
        loop(1, groups, lambda o: copy_d(half, other_group(o), my_group).wait_send())
        loop(1, groups, lambda o: copy_d(half, other_group(o), other_group(o)).wait_recv())

    loop(0, halves, receive)


def filter_bands(panel, potential, ritz, side, cells_x, cells_y, groups):
    chunks, doms, rows, bands, lanes = panel.shape
    total, part = doms * groups, rows // groups
    field = (side * cells_x, side * cells_y, bands, lanes)
    dma = pltpu.SemaphoreType.DMA
    blocks = (chunks, total, part, bands, lanes)
    fused = ritz is not None
    scratch = [
        pltpu.VMEM((doms,) + potential.shape, jnp.float32),
        pltpu.VMEM(panel.shape, jnp.bfloat16),
        pltpu.VMEM(panel.shape, jnp.bfloat16),
        pltpu.VMEM(field, jnp.float32),
        pltpu.VMEM(field, jnp.float32),
        dma((doms,)),
        dma((doms,)),
        dma,
        dma((chunks, doms)),
        dma((chunks, doms)),
        dma((chunks,)),
        dma((chunks, total)),
        dma((chunks, total)),
        dma((chunks,)),
    ]
    operands, result = (panel, potential), blocks
    if fused:
        _, wide, depth = ritz.shape
        pair = 2 if part % 2 == 0 else 1
        halves = part // pair
        operands, result = (panel, potential, ritz), (groups, part, wide, lanes)
        scratch += [
            pltpu.VMEM(blocks, jnp.bfloat16),
            pltpu.VMEM((QUARTERS, groups * wide, depth), jnp.bfloat16),
            pltpu.VMEM((halves, pair, groups * wide, lanes), jnp.bfloat16),
            dma((groups,)),
            dma((groups,)),
            dma,
            dma((3,)),
            dma((3,)),
            dma((halves, groups)),
            dma((halves, groups)),
            dma((halves,)),
        ]
    return pl.pallas_call(
        functools.partial(filter_kernel, side, cells_x, cells_y, doms, groups, fused),
        out_shape=jax.ShapeDtypeStruct(result, jnp.bfloat16),
        in_specs=[pl.BlockSpec(memory_space=pltpu.VMEM)] * len(operands),
        out_specs=pl.BlockSpec(memory_space=pltpu.VMEM),
        scratch_shapes=scratch,
        compiler_params=pltpu.CompilerParams(
            vmem_limit_bytes=40 * 2**20, collective_id=0, has_side_effects=True
        ),
        name="chebyshev",
    )(*operands)


def on_device(orbitals, potential, ritz):
    doms = lax.axis_size("dom")
    groups = lax.axis_size("band")
    side = math.isqrt(doms)
    bands, _, cells_x, cells_y, lanes = orbitals.shape
    rows = cells_x * cells_y
    share = bands // doms
    deep = min(share, 16)
    chunks = share // deep
    part = rows // groups
    panel = orbitals.reshape(doms, chunks, deep, rows, lanes).transpose(1, 0, 3, 2, 4)
    everyone = groups * bands
    if deep == 16 and chunks == 2 and doms == QUARTERS and everyone % 1024 == 0 and bands % 16 == 0:
        turned = ritz.reshape(groups, doms, chunks, deep, bands).transpose(4, 2, 0, 1, 3)
        turned = turned.reshape(bands, QUARTERS, everyone // QUARTERS).transpose(1, 0, 2)
        returned = filter_bands(
            panel, potential.reshape(rows, lanes), turned, side, cells_x, cells_y, groups
        )
        rotated = returned.transpose(2, 0, 1, 3).reshape(bands, rows, lanes)
        return rotated.astype(jnp.float32).reshape(orbitals.shape)
    full_ritz = lax.all_gather(ritz, "band", axis=1, tiled=True)
    block = filter_bands(panel, potential.reshape(rows, lanes), None, side, cells_x, cells_y, groups)
    block = block.reshape(chunks, groups * doms, part, deep, lanes).transpose(1, 0, 3, 2, 4)
    block = block.reshape(groups * bands, part * lanes)
    mixed = lax.dot_general(
        full_ritz, block, (((0,), (0,)), ((), ())), preferred_element_type=jnp.float32
    )
    mixed = mixed.astype(jnp.bfloat16).reshape(groups, bands, part, lanes)
    returned = lax.all_to_all(mixed, "band", split_axis=0, concat_axis=0, tiled=True)
    rotated = returned.transpose(1, 0, 2, 3).reshape(bands, rows, lanes)
    return rotated.astype(jnp.float32).reshape(orbitals.shape)


def solution(mesh):
    in_specs = (P("band", "dom", None, None, None), P("dom", None, None, None), P(None, "band"))
    out_specs = P("band", "dom", None, None, None)
    return jax.shard_map(
        on_device, mesh=mesh, in_specs=in_specs, out_specs=out_specs, check_vma=False
    )
```

```python
import functools
import math

import jax
import jax.numpy as jnp
from jax import lax
from jax.experimental import pallas as pl
from jax.experimental.pallas import tpu as pltpu
from jax.sharding import PartitionSpec as P

DEG = 4

lower_bound = -1.5
cut_off = 1.0
upper_bound = 9.5
coef_zero = -2.5
coef_one = 4.0 / 3.0
coef_two = -1.0 / 12.0


def filter_weights(degree):
    half_width = (upper_bound - cut_off) / 2.0
    centre = (upper_bound + cut_off) / 2.0
    sigma_now = half_width / (lower_bound - centre)
    first_scale = sigma_now / half_width
    inverse_gain = 2.0 / sigma_now
    weights = []
    for degree_step in range(1, degree):
        sigma_next = 1.0 / (inverse_gain - sigma_now)
        weights.append((2.0 * sigma_next / half_width, sigma_now * sigma_next))
        sigma_now = sigma_next
    return (centre, first_scale, weights)


def peer_of(index, doms):
    return {"band": lax.div(index, doms), "dom": lax.rem(index, doms)}


def loop(low, high, body, unroll=None):
    lax.fori_loop(low, high, lambda i, c: (body(i), c)[1], 0, unroll=unroll)


QUARTERS = 4


def filter_kernel(side, cells_x, cells_y, doms, groups, fused, *refs):
    if fused:
        panel, pot_in, ritz_in, final = refs[:4]
        out_ref, ritz_all, mixed, send_r, recv_r, here_r, send_x, recv_x, send_d, recv_d, here_d = refs[-11:]
        refs = refs[4:-11]
    else:
        panel, pot_in, out_ref = refs[:3]
        refs = refs[3:]
    pot_ref, got, done, even, odd = refs[:5]
    send_p, recv_p, here_p, send_a, recv_a, here_a, send_b, recv_b, here_b = refs[5:]
    chunks = panel.shape[0]
    count_x, count_y = even.shape[0], even.shape[1]
    part = out_ref.shape[2]
    total = doms * groups
    my_dom, my_group = lax.axis_index("dom"), lax.axis_index("band")
    me = my_group * doms + my_dom
    centre, first_scale, weights = filter_weights(DEG)
    diagonal = -0.5 * 3.0 * coef_zero - centre

    barrier = pltpu.get_barrier_semaphore()

    def greet(offset):
        pl.semaphore_signal(
            barrier, inc=1, device_id=peer_of(lax.rem(me + offset, total), doms),
            device_id_type=pl.DeviceIdType.MESH,
        )

    loop(1, total, greet)
    pl.semaphore_wait(barrier, total - 1)

    def copy_p(target, source):
        return pltpu.make_async_remote_copy(
            src_ref=pot_in,
            dst_ref=pot_ref.at[source],
            send_sem=send_p.at[target],
            recv_sem=recv_p.at[source],
            device_id={"dom": target},
            device_id_type=pl.DeviceIdType.MESH,
        )

    def copy_a(chunk, target, source):
        return pltpu.make_async_remote_copy(
            src_ref=panel.at[chunk, target],
            dst_ref=got.at[chunk, source],
            send_sem=send_a.at[chunk, target],
            recv_sem=recv_a.at[chunk, source],
            device_id={"dom": target},
            device_id_type=pl.DeviceIdType.MESH,
        )

    def copy_b(chunk, target, source):
        group, dom = lax.div(target, doms), lax.rem(target, doms)
        return pltpu.make_async_remote_copy(
            src_ref=done.at[chunk, dom, pl.ds(group * part, part)],
            dst_ref=out_ref.at[chunk, source],
            send_sem=send_b.at[chunk, target],
            recv_sem=recv_b.at[chunk, source],
            device_id=peer_of(target, doms),
            device_id_type=pl.DeviceIdType.MESH,
        )

    def local_a(chunk):
        return pltpu.make_async_copy(
            panel.at[chunk, my_dom], got.at[chunk, my_dom], here_a.at[chunk]
        )

    def local_b(chunk):
        return pltpu.make_async_copy(
            done.at[chunk, my_dom, pl.ds(my_group * part, part)],
            out_ref.at[chunk, me], here_b.at[chunk],
        )

    def other_dom(offset):
        return lax.rem(my_dom + offset, doms)

    def other(offset):
        return lax.rem(me + offset, total)

    def start_a(chunk):
        local_a(chunk).start()
        loop(1, doms, lambda o: copy_a(chunk, other_dom(o), my_dom).start())

    local_p = pltpu.make_async_copy(pot_in, pot_ref.at[my_dom], here_p)
    local_p.start()
    loop(1, doms, lambda o: copy_p(other_dom(o), my_dom).start())
    loop(0, chunks, start_a)
    if fused:
        wide = ritz_in.shape[1]
        quarter = lax.rem(my_dom, QUARTERS)
        base = my_dom - quarter
        across = lax.rem(quarter + 2, QUARTERS)
        beside = quarter + 1 - 2 * lax.rem(quarter, 2)
        opposite = lax.rem(beside + 2, QUARTERS)

        def other_group(offset):
            return lax.rem(my_group + offset, groups)

        def copy_r(target, source):
            return pltpu.make_async_remote_copy(
                src_ref=ritz_in.at[quarter],
                dst_ref=ritz_all.at[quarter, pl.ds(pl.multiple_of(source * wide, wide), wide)],
                send_sem=send_r.at[target],
                recv_sem=recv_r.at[source],
                device_id={"band": target},
                device_id_type=pl.DeviceIdType.MESH,
            )

        def copy_x(which, index, target):
            return pltpu.make_async_remote_copy(
                src_ref=ritz_all.at[index],
                dst_ref=ritz_all.at[index],
                send_sem=send_x.at[which],
                recv_sem=recv_x.at[which],
                device_id={"dom": base + target},
                device_id_type=pl.DeviceIdType.MESH,
            )

        local_r = pltpu.make_async_copy(
            ritz_in.at[quarter],
            ritz_all.at[quarter, pl.ds(pl.multiple_of(my_group * wide, wide), wide)],
            here_r,
        )
        local_r.start()
        loop(1, groups, lambda o: copy_r(other_group(o), my_group).start())
    local_p.wait()
    loop(1, doms, lambda o: copy_p(my_dom, other_dom(o)).wait_recv())

    def block_of(x, y):
        dom = (x // cells_x) * side + lax.div(y, cells_y)
        row = (x % cells_x) * cells_y + lax.rem(y, cells_y)
        return dom, row

    def load(chunk, y):
        for x in range(count_x):
            dom, row = block_of(x, y)
            even[x, y] = got[chunk, dom, row].astype(jnp.float32)

    def step(chunk, source, target, scale_h, scale_x, last):
        tall = 4 if cells_y % 4 == 0 else 1
        slab = min(8, even.shape[2])

        def slab_step(first, bands):
            ys = [lax.rem(first + (k - 2) + count_y, count_y) for k in range(tall + 4)]
            rows = [[source[x, y, bands] for y in ys] for x in range(count_x)]
            values = []
            for x in range(count_x):
                dom, row = block_of(x, first)
                for k in range(tall):
                    here = rows[x][k + 2]
                    side_near = rows[(x + 1) % count_x][k + 2] + rows[(x - 1) % count_x][k + 2]
                    side_far = rows[(x + 2) % count_x][k + 2] + rows[(x - 2) % count_x][k + 2]
                    near = (
                        side_near
                        + (rows[x][k + 1] + rows[x][k + 3])
                        + (pltpu.roll(here, 1, 1) + pltpu.roll(here, 127, 1))
                    )
                    far = (
                        side_far
                        + (rows[x][k] + rows[x][k + 4])
                        + (pltpu.roll(here, 2, 1) + pltpu.roll(here, 126, 1))
                    )
                    pot = (pot_ref[dom, pl.ds(row + k, 1), :] + diagonal) * scale_h
                    value = pot * here + (
                        (-0.5 * coef_one * scale_h) * near + (-0.5 * coef_two * scale_h) * far
                    )
                    if scale_x is not None:
                        value = value - scale_x * target[x, first + k, bands]
                    values.append((x, first + k, value))
            for x, y, value in values:
                target[x, y, bands] = value

        def block_step(block):
            for low in range(0, even.shape[2], slab):
                slab_step(block * tall, pl.ds(low, slab))

        loop(0, count_y // tall, block_step)
        if not last:
            return

        def pack(y):
            for x in range(count_x):
                dom, row = block_of(x, y)
                done[chunk, dom, row] = target[x, y].astype(done.dtype)

        loop(0, count_y, pack, unroll=4)

    def work(chunk):
        local_a(chunk).wait()
        loop(1, doms, lambda o: copy_a(chunk, my_dom, other_dom(o)).wait_recv())
        loop(0, count_y, lambda y: load(chunk, y), unroll=2)
        step(chunk, even, odd, first_scale, None, False)
        source, target = odd, even
        for index, (scale_h, scale_x) in enumerate(weights):
            step(chunk, source, target, scale_h, scale_x, index == len(weights) - 1)
            source, target = target, source
        loop(1, total, lambda o: copy_b(chunk, other(o), me).start())
        local_b(chunk).start()

    if fused:
        loop(0, 1, work)
        local_r.wait()
        loop(1, groups, lambda o: copy_r(my_group, other_group(o)).wait_recv())
        copy_x(0, quarter, across).start()
        copy_x(1, quarter, beside).start()
        loop(1, chunks, work)
        copy_x(0, across, across).wait_recv()
        copy_x(2, across, beside).start()
        loop(1, groups, lambda o: copy_r(other_group(o), my_group).wait_send())
        copy_x(1, beside, beside).wait_recv()
        copy_x(2, opposite, beside).wait_recv()
    else:
        loop(0, chunks, work)

    loop(1, doms, lambda o: copy_p(other_dom(o), my_dom).wait_send())

    def finish(chunk):
        loop(1, doms, lambda o: copy_a(chunk, other_dom(o), my_dom).wait_send())
        local_b(chunk).wait()
        loop(1, total, lambda o: copy_b(chunk, other(o), me).wait_send())
        loop(1, total, lambda o: copy_b(chunk, other(o), other(o)).wait_recv())

    loop(0, chunks, finish)
    if not fused:
        return
    copy_x(0, quarter, across).wait_send()
    copy_x(1, quarter, beside).wait_send()
    copy_x(2, across, beside).wait_send()

    halves, pair = mixed.shape[0], mixed.shape[1]
    deep, lanes = out_ref.shape[3], out_ref.shape[4]
    depth = ritz_all.shape[2]
    devices = depth // deep

    def copy_d(half, target, source):
        return pltpu.make_async_remote_copy(
            src_ref=mixed.at[half, :, pl.ds(pl.multiple_of(target * wide, wide), wide)],
            dst_ref=final.at[source, pl.ds(half * pair, pair)],
            send_sem=send_d.at[half, target],
            recv_sem=recv_d.at[half, source],
            device_id={"band": target},
            device_id_type=pl.DeviceIdType.MESH,
        )

    def local_d(half):
        return pltpu.make_async_copy(
            mixed.at[half, :, pl.ds(pl.multiple_of(my_group * wide, wide), wide)],
            final.at[my_group, pl.ds(half * pair, pair)], here_d.at[half],
        )

    for half in range(halves):
        columns = []
        for q in range(QUARTERS):
            chunk, first = (q * devices) // total, (q * devices) % total
            pieces = [
                out_ref[chunk, first : first + devices, half * pair + r].reshape(depth, lanes)
                for r in range(pair)
            ]
            columns.append(jnp.concatenate(pieces, axis=1))

        def rotate(g):
            rows = pl.ds(pl.multiple_of(g * 256, 256), 256)
            value = jnp.dot(ritz_all[0, rows, :], columns[0], preferred_element_type=jnp.float32)
            for q in range(1, QUARTERS):
                value = value + jnp.dot(
                    ritz_all[q, rows, :], columns[q], preferred_element_type=jnp.float32
                )
            for r in range(pair):
                mixed[half, r, rows, :] = value[:, r * lanes : (r + 1) * lanes].astype(mixed.dtype)

        for g in range(ritz_all.shape[1] // 256):
            rotate(g)
        loop(1, groups, lambda o: copy_d(half, other_group(o), my_group).start())
        local_d(half).start()

    def receive(half):
        local_d(half).wait()
        loop(1, groups, lambda o: copy_d(half, other_group(o), my_group).wait_send())
        loop(1, groups, lambda o: copy_d(half, other_group(o), other_group(o)).wait_recv())

    loop(0, halves, receive)


def filter_bands(panel, potential, ritz, side, cells_x, cells_y, groups):
    chunks, doms, rows, bands, lanes = panel.shape
    total, part = doms * groups, rows // groups
    field = (side * cells_x, side * cells_y, bands, lanes)
    dma = pltpu.SemaphoreType.DMA
    blocks = (chunks, total, part, bands, lanes)
    fused = ritz is not None
    scratch = [
        pltpu.VMEM((doms,) + potential.shape, jnp.float32),
        pltpu.VMEM(panel.shape, jnp.bfloat16),
        pltpu.VMEM(panel.shape, jnp.bfloat16),
        pltpu.VMEM(field, jnp.float32),
        pltpu.VMEM(field, jnp.float32),
        dma((doms,)),
        dma((doms,)),
        dma,
        dma((chunks, doms)),
        dma((chunks, doms)),
        dma((chunks,)),
        dma((chunks, total)),
        dma((chunks, total)),
        dma((chunks,)),
    ]
    operands, result = (panel, potential), blocks
    if fused:
        _, wide, depth = ritz.shape
        pair = 2 if part % 2 == 0 else 1
        halves = part // pair
        operands, result = (panel, potential, ritz), (groups, part, wide, lanes)
        scratch += [
            pltpu.VMEM(blocks, jnp.bfloat16),
            pltpu.VMEM((QUARTERS, groups * wide, depth), jnp.bfloat16),
            pltpu.VMEM((halves, pair, groups * wide, lanes), jnp.bfloat16),
            dma((groups,)),
            dma((groups,)),
            dma,
            dma((3,)),
            dma((3,)),
            dma((halves, groups)),
            dma((halves, groups)),
            dma((halves,)),
        ]
    return pl.pallas_call(
        functools.partial(filter_kernel, side, cells_x, cells_y, doms, groups, fused),
        out_shape=jax.ShapeDtypeStruct(result, jnp.bfloat16),
        in_specs=[pl.BlockSpec(memory_space=pltpu.VMEM)] * len(operands),
        out_specs=pl.BlockSpec(memory_space=pltpu.VMEM),
        scratch_shapes=scratch,
        compiler_params=pltpu.CompilerParams(
            vmem_limit_bytes=40 * 2**20, collective_id=0, has_side_effects=True
        ),
        name="chebyshev",
    )(*operands)


def on_device(orbitals, potential, ritz):
    doms = lax.axis_size("dom")
    groups = lax.axis_size("band")
    side = math.isqrt(doms)
    bands, _, cells_x, cells_y, lanes = orbitals.shape
    rows = cells_x * cells_y
    share = bands // doms
    deep = min(share, 16)
    chunks = share // deep
    part = rows // groups
    panel = orbitals.reshape(doms, chunks, deep, rows, lanes).transpose(1, 0, 3, 2, 4)
    everyone = groups * bands
    if deep == 16 and chunks == 2 and doms == QUARTERS and everyone % 1024 == 0 and bands % 16 == 0:
        turned = ritz.reshape(groups, doms, chunks, deep, bands).transpose(4, 2, 0, 1, 3)
        turned = turned.reshape(bands, QUARTERS, everyone // QUARTERS).transpose(1, 0, 2)
        returned = filter_bands(
            panel, potential.reshape(rows, lanes), turned, side, cells_x, cells_y, groups
        )
        rotated = returned.transpose(2, 0, 1, 3).reshape(bands, rows, lanes)
        return rotated.astype(jnp.float32).reshape(orbitals.shape)
    full_ritz = lax.all_gather(ritz, "band", axis=1, tiled=True)
    block = filter_bands(panel, potential.reshape(rows, lanes), None, side, cells_x, cells_y, groups)
    block = block.reshape(chunks, groups * doms, part, deep, lanes).transpose(1, 0, 3, 2, 4)
    block = block.reshape(groups * bands, part * lanes)
    mixed = lax.dot_general(
        full_ritz, block, (((0,), (0,)), ((), ())), preferred_element_type=jnp.float32
    )
    mixed = mixed.astype(jnp.bfloat16).reshape(groups, bands, part, lanes)
    returned = lax.all_to_all(mixed, "band", split_axis=0, concat_axis=0, tiled=True)
    rotated = returned.transpose(1, 0, 2, 3).reshape(bands, rows, lanes)
    return rotated.astype(jnp.float32).reshape(orbitals.shape)


def solution(mesh):
    in_specs = (P("band", "dom", None, None, None), P("dom", None, None, None), P(None, "band"))
    out_specs = P("band", "dom", None, None, None)
    return jax.shard_map(
        on_device, mesh=mesh, in_specs=in_specs, out_specs=out_specs, check_vma=False
    )
```
